32 devices in a mesh: job: 2 (over y), fsdp: 8 (over z, x), tp: 2 (over core).
Axes of the slice: x: 2, y: 2, z: 4, core: 2. Of those that a mesh axis runs over, the one named last changes fastest.
Arguments:
- weight: bfloat16 [8192, 16384], P(('job', 'fsdp'), 'tp'), parts along dimension 0, may hold values from -0.09375 to 0.09375
- grad: bfloat16 [8192, 16384], P(('job', 'fsdp'), 'tp'), parts along dimension 0, may hold values from -36 to 36
- row_moment: float32 [8192], P(('job', 'fsdp')), parts along dimension 0, may hold values from 0.01 to 10
- col_moment: float32 [32768], P(('job', 'tp')), parts along dimension 0, may hold values from 0.01 to 10
- states: bfloat16 [768, 4096], P(('job', 'fsdp')), parts along dimension 0, may hold values from -6 to 6
- norm_gain: bfloat16 [8192], P('job'), parts along dimension 0, may hold values from 0.099609375 to 1.8984375
- gate_values: bfloat16 [768, 16384], P(('job', 'fsdp'), 'tp'), parts along dimension 0, may hold values from -8 to 8
Outputs:
- new_weight: bfloat16 [8192, 16384], P(('job', 'fsdp'), 'tp'), parts along dimension 0
- new_rows: float32 [8192], P(('job', 'fsdp')), parts along dimension 0
- new_columns: float32 [32768], P(('job', 'tp')), parts along dimension 0
- hidden: bfloat16 [768, 16384], P(('job', 'fsdp'), 'tp'), parts along dimension 0
The draws below stay inside these ranges and needn't reach their ends.
There are 2 independent parts, one for each index of `job`. The reference program is written for one: setup_inputs(seed, part) draws one part's arguments, and reference() takes and returns one part's arrays. A program takes and returns all parts, laid end to end along the dimension named above; each array names one. Nothing has to cross between parts.
All inputs are finite; a program needn't handle non-finite values.
Results may differ from the reference program's by a relative error of at most 0.002.
The reference program's roundings to bfloat16 on the way (of `normed` and `up_values`) count: a program that leaves them out, or rounds other values in their place, can miss the bound.
Values may be sent and summed in bfloat16 or wider, within the bound.
A program may use at most 128 MiB of HBM per device.

```python
import math
import jax
import jax.numpy as jnp
from jax import lax

D = 4096
FF = 16384
TOKENS = 384


def draw_grad(key, part):
    row_key, col_key, random_key = jax.random.split(key, 3)
    row_place = jnp.arange(D).astype(jnp.float32) / (D - 1)
    col_place = jnp.arange(FF).astype(jnp.float32) / (FF - 1)
    row_draw = jax.random.uniform(row_key, (D,), jnp.float32)
    col_draw = jax.random.uniform(col_key, (FF,), jnp.float32)
    row_scale = 0.1 * jnp.exp(math.log(10.0) * row_draw + math.log(3.0) * row_place)
    col_scale = 0.1 * jnp.exp(math.log(10.0) * col_draw + math.log(3.0) * col_place)
    random_part = jax.random.truncated_normal(random_key, -4.0, 4.0, (D, FF), jnp.float32)
    return (random_part * row_scale[:, None] * col_scale[None, :]).astype(jnp.bfloat16)


def block_scale(stream_key, shape, pieces, smallest, top_value):
    gain, own = 1.0, jax.random.fold_in(stream_key, 6)
    for position, shards_of in pieces:
        heights = jnp.exp(jax.random.uniform(jax.random.fold_in(own, position), (shards_of,), jnp.float32, smallest / len(pieces), top_value / len(pieces)))
        gain = gain * jnp.repeat(heights, shape[position] // shards_of).reshape([-1 if axis == position else 1 for axis in range(len(shape))])
    return gain


def normal_values(rng, extent, deviation, bound, pieces=(), dtype=jnp.bfloat16):
    loudness = block_scale(rng, extent, pieces, -0.22, 0.18) if pieces else 1.0
    drawn = jax.random.normal(rng, extent, jnp.float32) * deviation * loudness
    return jnp.minimum(jnp.maximum(drawn, -bound), bound).astype(dtype)


def setup_inputs(seed: int = 0, part: int = 0) -> dict:
    seeds = jax.random.split(jax.random.key(seed), 8)
    own_keys = jax.random.split(jax.random.fold_in(seeds[7], part), 8)
    weight = normal_values(own_keys[0], (D, FF), D ** -0.5, 0.09375, ((0, 8), (1, 2)))
    grad = draw_grad(jax.random.fold_in(jax.random.fold_in(seeds[7], part), 71), part)
    row_moment = jnp.clip(jnp.exp(math.log(10.0) - 6.9077553 * jax.random.uniform(own_keys[2], (D,), jnp.float32) ** block_scale(own_keys[2], (D,), ((0, 8),), -0.2, 0.2)), 0.01, 10.0)
    col_moment = jnp.clip(jnp.exp(math.log(10.0) - 6.9077553 * jax.random.uniform(own_keys[3], (FF,), jnp.float32) ** block_scale(own_keys[3], (FF,), ((0, 2),), -0.2, 0.2)), 0.01, 10.0)
    states = normal_values(own_keys[4], (TOKENS, D), 1.0, 6.0, ((0, 8),))
    norm_gain = jnp.clip(1.0 + 0.18 * jax.random.normal(own_keys[5], (D,), jnp.float32), 0.099609375, 1.8984375).astype(jnp.bfloat16)
    gate_values = normal_values(own_keys[6], (TOKENS, FF), 2.0, 8.0, ((0, 8), (1, 2)))
    return {"weight": weight, "grad": grad, "row_moment": row_moment, "col_moment": col_moment, "states": states, "norm_gain": norm_gain, "gate_values": gate_values}


def reference(weight, grad, row_moment, col_moment, states, norm_gain, gate_values):
    gradient = grad.astype(jnp.float32)
    squares = gradient * gradient + 1e-30
    row_mean = lax.optimization_barrier(jnp.mean(squares, axis=1))
    col_mean = lax.optimization_barrier(jnp.mean(squares, axis=0))
    new_rows = 0.8 * row_moment + 0.2 * row_mean
    new_columns = 0.8 * col_moment + 0.2 * col_mean
    row_scale = jnp.mean(new_rows)
    update = gradient / jnp.sqrt(new_rows[:, None] * new_columns[None, :] / row_scale)
    new_weight = (weight.astype(jnp.float32) - 0.01 * update).astype(jnp.bfloat16)
    values = states.astype(jnp.float32)
    normed = (values * lax.rsqrt(lax.optimization_barrier(jnp.mean(values * values, axis=1, keepdims=True)) + 1e-06) * norm_gain.astype(jnp.float32)).astype(jnp.bfloat16)
    up_values = jnp.dot(normed, new_weight, preferred_element_type=jnp.float32).astype(jnp.bfloat16)
    hidden = (jax.nn.silu(gate_values.astype(jnp.float32)) * up_values.astype(jnp.float32)).astype(jnp.bfloat16)
    return (new_weight, new_rows, new_columns, hidden)
```

```python
import functools
import jax
import jax.numpy as jnp
from jax import lax
from jax.experimental import pallas as pl
from jax.experimental.pallas import tpu as pltpu
from jax.sharding import PartitionSpec as P

MESH = pl.DeviceIdType.MESH
F32 = jnp.float32
BF16 = jnp.bfloat16
LANES = 128
CHUNKS = 8
POWER = 9
VMEM_BUDGET = 56 * 1024 * 1024
GAIN_MAX = 1.8984375


def stats_kernel(
    n, ff, d_model,
    grad_ref, weight_ref, row_moment_ref, col_moment_ref, states_ref, gain_ref,
    rows_ref, cols_ref, row_factor_ref, col_factor_ref, scale_ref, normed_ref,
    grad_buf, weight_buf, row_acc, row_buf, row_recv, col_buf, col_recv, msg, all_buf,
    norm_buf, norm_got,
    load_sem, wload_sem, row_sems, col_send, col_recv_sem, msg_send, msg_recv,
    norm_send, norm_recv, pass_sems,
):
    me = lax.axis_index("fsdp")
    core = lax.axis_index("tp")
    rows, cols = grad_ref.shape
    pieces = grad_buf.shape[0]
    width = cols // pieces
    groups = width // LANES
    chunk = cols // n // LANES
    row_groups = rows // LANES

    def load(p):
        return pltpu.make_async_copy(
            grad_ref.at[:, pl.ds(pl.multiple_of(p * width, LANES), width)],
            grad_buf.at[p],
            load_sem.at[p],
        )

    for p in range(pieces):
        load(p).start()
    wload = pltpu.make_async_copy(weight_ref, weight_buf, wload_sem)
    wload.start()

    barrier = pltpu.get_barrier_semaphore()
    for d in range(1, n):
        pl.semaphore_signal(
            barrier, inc=1, device_id={"fsdp": lax.rem(me + d, n)}, device_id_type=MESH
        )
    pl.semaphore_signal(barrier, inc=1, device_id={"tp": 1 - core}, device_id_type=MESH)

    values = states_ref[...].astype(F32)
    inverse = lax.rsqrt(jnp.mean(values * values, axis=1, keepdims=True) + 1e-06)
    normed = (values * inverse * gain_ref[...].astype(F32)).astype(BF16)
    half = rows // 2
    for p in range(n):
        for h in range(2):
            at = p * rows + h * half
            norm_buf[h, p] = normed[:, at : at + half]
    pl.semaphore_wait(barrier, n)

    def send_normed(d):
        peer = lax.rem(me + d, n)
        return pltpu.make_async_remote_copy(
            src_ref=norm_buf.at[core, peer],
            dst_ref=norm_got.at[core, me],
            send_sem=norm_send.at[d],
            recv_sem=norm_recv.at[d],
            device_id={"fsdp": peer},
            device_id_type=MESH,
        )

    for d in range(1, n):
        send_normed(d).start()
    norm_got[core, me] = norm_buf[core, me]

    row_acc[...] = jnp.zeros_like(row_acc)
    step_rows = 32

    @pl.loop(0, pieces)
    def _(p):
        load(p).wait()

        def body(r, acc):
            at = pl.multiple_of(r * step_rows, step_rows)
            x = grad_buf[p, pl.ds(at, step_rows), :].astype(F32)
            sq = x * x
            lane = sq[:, :LANES]
            for g in range(1, groups):
                lane = lane + sq[:, g * LANES : (g + 1) * LANES]
            row_acc[pl.ds(at, step_rows), :] += lane
            return acc + jnp.sum(sq.reshape(step_rows // 8, 8, width), axis=0)

        acc = lax.fori_loop(0, rows // step_rows, body, jnp.zeros((8, width), F32))
        total = jnp.sum(acc, axis=0, keepdims=True)
        for g in range(groups):
            col_buf[p, g : g + 1, :] = total[:, g * LANES : (g + 1) * LANES]

    row_line = jnp.sum(jnp.transpose(row_acc[...]), axis=0, keepdims=True)
    row_buf[...] = jnp.zeros_like(row_buf)
    for g in range(row_groups):
        row_buf[g : g + 1, :] = row_line[:, g * LANES : (g + 1) * LANES]

    send_rows = pltpu.make_async_remote_copy(
        src_ref=row_buf, dst_ref=row_recv, send_sem=row_sems.at[0], recv_sem=row_sems.at[1],
        device_id={"tp": 1 - core}, device_id_type=MESH,
    )

    def send_cols(d):
        peer = lax.rem(me + d, n)
        return pltpu.make_async_remote_copy(
            src_ref=col_buf.at[peer], dst_ref=col_recv.at[d],
            send_sem=col_send.at[d], recv_sem=col_recv_sem.at[d],
            device_id={"fsdp": peer}, device_id_type=MESH,
        )

    send_rows.start()
    for d in range(1, n):
        send_cols(d).start()

    wload.wait()

    def biggest(r, m):
        x = jnp.abs(weight_buf[pl.ds(pl.multiple_of(r * 16, 16), 16), :])
        for g in range(cols // LANES):
            m = jnp.maximum(m, x[:, g * LANES : (g + 1) * LANES])
        return m

    weight_max = lax.fori_loop(0, rows // 16, biggest, jnp.zeros((16, LANES), BF16))
    weight_max = jnp.max(weight_max.astype(F32), axis=(0, 1), keepdims=True)

    send_rows.wait()
    row_total = row_buf[...] + row_recv[...]
    new_rows = 0.8 * row_moment_ref[...] + 0.2 * (row_total[:row_groups] / ff + 1e-30)
    rows_ref[...] = new_rows
    rows_summed = jnp.sum(new_rows, axis=(0, 1), keepdims=True)
    rows_least = jnp.min(new_rows, axis=(0, 1), keepdims=True)

    col_total = col_buf[me]
    for d in range(1, n):
        send_cols(d).wait()
        col_total = col_total + col_recv[d]
    msg[0:chunk] = col_total
    msg[chunk : chunk + 8] = jnp.zeros((8, LANES), F32)
    msg[chunk : chunk + 1] = jnp.broadcast_to(rows_summed, (1, LANES))
    msg[chunk + 1 : chunk + 2] = jnp.broadcast_to(rows_least, (1, LANES))
    msg[chunk + 2 : chunk + 3] = jnp.broadcast_to(weight_max, (1, LANES))

    def send_msg(d):
        return pltpu.make_async_remote_copy(
            src_ref=msg, dst_ref=all_buf.at[me],
            send_sem=msg_send.at[d], recv_sem=msg_recv.at[d],
            device_id={"fsdp": lax.rem(me + d, n)}, device_id_type=MESH,
        )

    for d in range(1, n):
        send_msg(d).start()
    all_buf[me] = msg[...]

    for d in range(1, n):
        send_normed(d).wait()
    give = pltpu.make_async_remote_copy(
        src_ref=norm_got.at[core], dst_ref=norm_got.at[core],
        send_sem=pass_sems.at[0], recv_sem=pass_sems.at[1],
        device_id={"tp": 1 - core}, device_id_type=MESH,
    )
    give.start()

    for d in range(1, n):
        send_msg(d).wait()
    summed = all_buf[0, chunk : chunk + 1, :]
    least = all_buf[0, chunk + 1 : chunk + 2, :]
    heaviest = all_buf[0, chunk + 2 : chunk + 3, :]
    for o in range(1, n):
        summed = summed + all_buf[o, chunk : chunk + 1, :]
        least = jnp.minimum(least, all_buf[o, chunk + 1 : chunk + 2, :])
        heaviest = jnp.maximum(heaviest, all_buf[o, chunk + 2 : chunk + 3, :])
    row_scale = summed / d_model
    ratio = jnp.zeros((1, LANES), F32)
    for o in range(n):
        here = slice(o * chunk, (o + 1) * chunk)
        sums = all_buf[o, 0:chunk, :]
        new_columns = 0.8 * col_moment_ref[here, :] + 0.2 * (sums / d_model + 1e-30)
        cols_ref[here, :] = new_columns
        col_factor_ref[here, :] = lax.rsqrt(new_columns)
        ratio = jnp.maximum(ratio, jnp.max(sums / new_columns, axis=0, keepdims=True))
    ratio = jnp.max(ratio, axis=1, keepdims=True)
    factor = 0.01 * jnp.sqrt(row_scale[:, 0:1]) * lax.rsqrt(new_rows)
    for g in range(row_groups):
        line = jnp.broadcast_to(factor[g : g + 1, :], (LANES, LANES))
        row_factor_ref[g * LANES : (g + 1) * LANES, :] = jnp.transpose(line)

    column_norm = d_model**0.5 * heaviest + 0.01 * jnp.sqrt(row_scale / least * ratio)
    bound = 1.02 * GAIN_MAX * d_model**0.5 * column_norm + 1e-25
    scale_ref[...] = jnp.zeros_like(scale_ref)
    scale_ref[0:1, :] = 8000.0 / bound
    scale_ref[1:2, :] = bound / 8000.0

    give.wait()
    normed_ref[...] = norm_got[...]


def statistics(n, ff, d_model, grad, weight, row_moment, col_moment, states, gain):
    rows, cols = grad.shape
    tokens = states.shape[0]
    chunk = cols // n // LANES
    half = rows // 2
    vmem = pl.BlockSpec(memory_space=pltpu.VMEM)
    hbm = pl.BlockSpec(memory_space=pl.ANY)
    shape = jax.ShapeDtypeStruct
    dma = pltpu.SemaphoreType.DMA
    return pl.pallas_call(
        functools.partial(stats_kernel, n, ff, d_model),
        out_shape=(
            shape((rows // LANES, LANES), F32),
            shape((cols // LANES, LANES), F32),
            shape((rows, LANES), F32),
            shape((cols // LANES, LANES), F32),
            shape((8, LANES), F32),
            shape((2, n, tokens, half), BF16),
        ),
        in_specs=[hbm, hbm, vmem, vmem, vmem, vmem],
        out_specs=(vmem,) * 6,
        scratch_shapes=[
            pltpu.VMEM((n, rows, cols // n), BF16),
            pltpu.VMEM((rows, cols), BF16),
            pltpu.VMEM((rows, LANES), F32),
            pltpu.VMEM((8, LANES), F32),
            pltpu.VMEM((8, LANES), F32),
            pltpu.VMEM((n, chunk, LANES), F32),
            pltpu.VMEM((n, chunk, LANES), F32),
            pltpu.VMEM((chunk + 8, LANES), F32),
            pltpu.VMEM((n, chunk + 8, LANES), F32),
            pltpu.VMEM((2, n, tokens, half), BF16),
            pltpu.VMEM((2, n, tokens, half), BF16),
            dma((n,)), dma, dma((2,)), dma((n,)), dma((n,)), dma((n,)), dma((n,)),
            dma((n,)), dma((n,)), dma((2,)),
        ],
        compiler_params=pltpu.CompilerParams(
            collective_id=0, has_side_effects=True, vmem_limit_bytes=VMEM_BUDGET
        ),
        name="statistics",
    )(
        grad, weight, row_moment.reshape(rows // LANES, LANES),
        col_moment.reshape(cols // LANES, LANES), states, gain.reshape(1, -1),
    )


def update_kernel(grad_ref, weight_ref, row_factor_ref, col_factor_ref, out_ref):
    for g in range(grad_ref.shape[1] // LANES):
        at = slice(g * LANES, (g + 1) * LANES)
        step = grad_ref[:, at].astype(F32) * row_factor_ref[...] * col_factor_ref[g : g + 1, :]
        out_ref[:, at] = (weight_ref[:, at].astype(F32) - step).astype(BF16)


def update(grad, weight, row_factor, col_factor):
    rows, cols = grad.shape
    width = 8 * LANES
    block = pl.BlockSpec((rows, width), lambda j: (0, j))
    return pl.pallas_call(
        update_kernel,
        grid=(cols // width,),
        out_shape=jax.ShapeDtypeStruct((rows, cols), BF16),
        in_specs=[
            block, block,
            pl.BlockSpec((rows, LANES), lambda j: (0, 0)),
            pl.BlockSpec((8, LANES), lambda j: (j, 0)),
        ],
        out_specs=block,
        compiler_params=pltpu.CompilerParams(vmem_limit_bytes=VMEM_BUDGET),
        name="update",
    )(grad, weight, row_factor, col_factor)


def encode(v):
    square = v * v
    fourth = square * square
    return (fourth * fourth * v).astype(BF16)


def decode(code, unscale):
    c = code.astype(F32)
    size = jnp.exp2(jnp.log2(jnp.abs(c)) * (1.0 / POWER)) * unscale
    return jnp.where(c < 0, -size, size)


def ring_kernel(
    n, weight_ref, normed_ref, gate_ref, scale_ref, out_ref,
    weight_buf, part, sent, got, load_sem, send_sem, recv_sem,
):
    steps = n // 2
    width = weight_buf.shape[2]
    tokens, half = normed_ref.shape[2], normed_ref.shape[3]
    index = lax.axis_index("fsdp")

    place = jnp.where(lax.rem(index, 2) == 0, index // 2, n - 1 - index // 2)

    def device_at(q):
        q = lax.rem(q + n, n)
        return jnp.where(q < n // 2, 2 * q, 2 * (n - 1 - q) + 1)

    neighbours = (device_at(place + 1), device_at(place - 1))

    def load(c):
        return pltpu.make_async_copy(
            weight_ref.at[:, pl.ds(pl.multiple_of(c * width, LANES), width)],
            weight_buf.at[c],
            load_sem.at[c],
        )

    for c in range(CHUNKS):
        load(c).start()

    barrier = pltpu.get_barrier_semaphore()
    for other in neighbours:
        pl.semaphore_signal(barrier, inc=1, device_id={"fsdp": other}, device_id_type=MESH)
    pl.semaphore_wait(barrier, 2)

    scale = scale_ref[0:1, 0:1]
    unscale = scale_ref[1:2, 0:1]

    def copy(way, step, c):
        return pltpu.make_async_remote_copy(
            src_ref=sent.at[way, step, c],
            dst_ref=got.at[way, step, c],
            send_sem=send_sem.at[way, step, c],
            recv_sem=recv_sem.at[way, step, c],
            device_id={"fsdp": neighbours[way]},
            device_id_type=MESH,
        )

    def pass_on(way, step, c, first):
        far = steps - step
        dest = device_at(place + far) if way == 0 else device_at(place - far)
        total = part[c, dest]
        if not first:
            copy(way, step - 1, c).wait_recv()
            total = total + decode(got[way, step - 1, c], unscale)
        sent[way, step, c] = encode(total * scale)
        copy(way, step, c).start()

    @pl.loop(0, CHUNKS // 2)
    def _(pair):
        for way in range(2):
            c = 2 * pair + way
            load(c).wait()
            product = jnp.dot(
                normed_ref[0].reshape(n * tokens, half), weight_buf[c, :half, :],
                preferred_element_type=F32,
            ) + jnp.dot(
                normed_ref[1].reshape(n * tokens, half), weight_buf[c, half:, :],
                preferred_element_type=F32,
            )
            part[c] = product.reshape(n, tokens, width)
            pass_on(way, 0, c, True)

    for step in range(1, steps):

        @pl.loop(0, CHUNKS // 2)
        def _(pair):
            for parity in range(2):
                for way in range(2):
                    pass_on(way, step, 2 * pair + parity, step == 1 and parity != way)

    @pl.loop(0, CHUNKS)
    def _(c):
        total = part[c, index]
        for way in range(2):
            copy(way, steps - 1, c).wait_recv()
            total = total + decode(got[way, steps - 1, c], unscale)
        up_values = total.astype(BF16).astype(F32)
        at = pl.ds(pl.multiple_of(c * width, LANES), width)
        gate = gate_ref[:, at].astype(F32)
        out_ref[:, at] = (gate / (1.0 + jnp.exp(-gate)) * up_values).astype(BF16)

    @pl.loop(0, CHUNKS // 2)
    def _(pair):
        for way in range(2):
            copy(way, 0, 2 * pair + way).wait_send()
            for step in range(1, steps):
                for parity in range(2):
                    copy(way, step, 2 * pair + parity).wait_send()


def project(n, weight, normed, gate, scale):
    rows, cols = weight.shape
    tokens = gate.shape[0]
    width = cols // CHUNKS
    vmem = pl.BlockSpec(memory_space=pltpu.VMEM)
    dma = pltpu.SemaphoreType.DMA
    slots = (2, n // 2, CHUNKS)
    return pl.pallas_call(
        functools.partial(ring_kernel, n),
        out_shape=jax.ShapeDtypeStruct(gate.shape, BF16),
        in_specs=[pl.BlockSpec(memory_space=pl.ANY), vmem, vmem, vmem],
        out_specs=vmem,
        scratch_shapes=[
            pltpu.VMEM((CHUNKS, rows, width), BF16),
            pltpu.VMEM((CHUNKS, n, tokens, width), F32),
            pltpu.VMEM((*slots, tokens, width), BF16),
            pltpu.VMEM((*slots, tokens, width), BF16),
            dma((CHUNKS,)), dma(slots), dma(slots),
        ],
        compiler_params=pltpu.CompilerParams(
            collective_id=1, has_side_effects=True, vmem_limit_bytes=VMEM_BUDGET
        ),
        name="project",
    )(weight, normed, gate, scale)


def kernels_fit(n, tp, rows, cols, tokens):
    ring = rows * cols * 2 + n * tokens * cols * (4 + 2 + 2) + 2 * tokens * cols * 2
    first = 2 * rows * cols * 2 + 4 * n * tokens * rows * 2 + 8 * tokens * n * rows * 4
    return (
        tp == 2
        and n >= 4
        and n % 2 == 0
        and rows % (2 * LANES) == 0
        and rows // LANES <= 8
        and cols % (8 * LANES * n) == 0
        and cols % (LANES * CHUNKS) == 0
        and tokens % 16 == 0
        and max(ring, first) <= VMEM_BUDGET - (8 << 20)
    )


def with_kernels(n, ff, d_model, weight, grad, row_moment, col_moment, states, gain, gate):
    new_rows, new_columns, row_factor, col_factor, scale, normed = statistics(
        n, ff, d_model, grad, weight, row_moment, col_moment, states, gain
    )
    new_weight = update(grad, weight, row_factor, col_factor)
    hidden = project(n, new_weight, normed, gate, scale)
    return new_weight, new_rows.reshape(-1), new_columns.reshape(-1), hidden


def with_collectives(ff, d_model, weight, grad, row_moment, col_moment, states, gain, gate):
    gradient = grad.astype(F32)
    squares = gradient * gradient + 1e-30
    row_total = lax.psum(jnp.sum(squares, axis=1), "tp")
    new_rows = 0.8 * row_moment + 0.2 * (row_total / ff)
    col_total, rows_summed = lax.psum((jnp.sum(squares, axis=0), jnp.sum(new_rows)), "fsdp")
    new_columns = 0.8 * col_moment + 0.2 * (col_total / d_model)
    row_scale = rows_summed / d_model
    change = gradient / jnp.sqrt(new_rows[:, None] * new_columns[None, :] / row_scale)
    new_weight = (weight.astype(F32) - 0.01 * change).astype(BF16)
    values = states.astype(F32)
    normed = (
        values
        * lax.rsqrt(jnp.mean(values * values, axis=1, keepdims=True) + 1e-06)
        * gain.astype(F32)
    ).astype(BF16)
    column_block = lax.all_to_all(new_weight, "fsdp", split_axis=1, concat_axis=0, tiled=True)
    up_block = jnp.dot(
        lax.all_gather(normed, "fsdp", axis=0, tiled=True),
        column_block,
        preferred_element_type=F32,
    ).astype(BF16)
    up_values = lax.all_to_all(up_block, "fsdp", split_axis=0, concat_axis=1, tiled=True)
    hidden = (jax.nn.silu(gate.astype(F32)) * up_values.astype(F32)).astype(BF16)
    return new_weight, new_rows, new_columns, hidden


def solution(mesh):
    n, tp = mesh.shape["fsdp"], mesh.shape["tp"]

    def on_device(weight, grad, row_moment, col_moment, states, gain, gate):
        rows, cols = weight.shape
        ff, d_model = cols * tp, rows * n
        arrays = (weight, grad, row_moment, col_moment, states, gain, gate)
        if kernels_fit(n, tp, rows, cols, states.shape[0]):
            return with_kernels(n, ff, d_model, *arrays)
        return with_collectives(ff, d_model, *arrays)

    return jax.shard_map(
        on_device,
        mesh=mesh,
        in_specs=(
            P(("job", "fsdp"), "tp"),
            P(("job", "fsdp"), "tp"),
            P(("job", "fsdp")),
            P(("job", "tp")),
            P(("job", "fsdp"), None),
            P("job"),
            P(("job", "fsdp"), "tp"),
        ),
        out_specs=(
            P(("job", "fsdp"), "tp"),
            P(("job", "fsdp")),
            P(("job", "tp")),
            P(("job", "fsdp"), "tp"),
        ),
        check_vma=False,
    )
```

```python
import functools
import jax
import jax.numpy as jnp
from jax import lax
from jax.experimental import pallas as pl
from jax.experimental.pallas import tpu as pltpu
from jax.sharding import PartitionSpec as P

MESH = pl.DeviceIdType.MESH
F32 = jnp.float32
BF16 = jnp.bfloat16
LANES = 128
CHUNKS = 8
POWER = 9
VMEM_BUDGET = 56 * 1024 * 1024
GAIN_MAX = 1.8984375


def encode(v):
    square = v * v
    fourth = square * square
    return (fourth * fourth * v).astype(BF16)


def decode(code, unscale):
    c = code.astype(F32)
    size = jnp.exp2(jnp.log2(jnp.abs(c)) * (1.0 / POWER)) * unscale
    return jnp.where(c < 0, -size, size)


def step_kernel(
    n, ff, d_model,
    grad_ref, weight_ref, row_moment_ref, col_moment_ref, states_ref, gain_ref,
    new_weight_ref, rows_ref, cols_ref, up_ref,
    grad_buf, weight_buf, row_acc, row_buf, row_recv, col_buf, col_recv, msg, all_buf,
    norm_buf, norm_got, row_factor, col_factor, part, sent, got,
    load_sem, wload_sem, store_sem, row_sems, col_send, col_recv_sem, msg_send, msg_recv,
    norm_send, norm_recv, pass_sems, send_sem, recv_sem,
):
    me = lax.axis_index("fsdp")
    core = lax.axis_index("tp")
    rows, cols = grad_ref.shape
    width = cols // CHUNKS
    groups = width // LANES
    chunk = cols // n // LANES
    row_groups = rows // LANES
    tokens = states_ref.shape[0]
    half = rows // 2
    steps = n // 2

    def columns(c):
        return pl.ds(pl.multiple_of(c * width, LANES), width)

    def load(c):
        return pltpu.make_async_copy(grad_ref.at[:, columns(c)], grad_buf.at[c], load_sem.at[c])

    def wload(c):
        return pltpu.make_async_copy(
            weight_ref.at[:, columns(c)], weight_buf.at[c], wload_sem.at[c]
        )

    def store(c):
        return pltpu.make_async_copy(
            weight_buf.at[c], new_weight_ref.at[:, columns(c)], store_sem.at[c]
        )

    for c in range(CHUNKS):
        load(c).start()
    for c in range(CHUNKS):
        wload(c).start()

    barrier = pltpu.get_barrier_semaphore()
    for d in range(1, n):
        pl.semaphore_signal(
            barrier, inc=1, device_id={"fsdp": lax.rem(me + d, n)}, device_id_type=MESH
        )
    pl.semaphore_signal(barrier, inc=1, device_id={"tp": 1 - core}, device_id_type=MESH)

    values = states_ref[...].astype(F32)
    inverse = lax.rsqrt(jnp.mean(values * values, axis=1, keepdims=True) + 1e-06)
    normed = (values * inverse * gain_ref[...].astype(F32)).astype(BF16)
    for p in range(n):
        for h in range(2):
            at = p * rows + h * half
            norm_buf[h, p] = normed[:, at : at + half]
    pl.semaphore_wait(barrier, n)

    def send_normed(d):
        peer = lax.rem(me + d, n)
        return pltpu.make_async_remote_copy(
            src_ref=norm_buf.at[core, peer],
            dst_ref=norm_got.at[core, me],
            send_sem=norm_send.at[d],
            recv_sem=norm_recv.at[d],
            device_id={"fsdp": peer},
            device_id_type=MESH,
        )

    for d in range(1, n):
        send_normed(d).start()
    norm_got[core, me] = norm_buf[core, me]

    row_acc[...] = jnp.zeros_like(row_acc)
    step_rows = 32

    @pl.loop(0, CHUNKS)
    def _(c):
        load(c).wait()

        def body(r, acc):
            at = pl.multiple_of(r * step_rows, step_rows)
            x = grad_buf[c, pl.ds(at, step_rows), :].astype(F32)
            sq = x * x
            lane = sq[:, :LANES]
            for g in range(1, groups):
                lane = lane + sq[:, g * LANES : (g + 1) * LANES]
            row_acc[pl.ds(at, step_rows), :] += lane
            return acc + jnp.sum(sq.reshape(step_rows // 8, 8, width), axis=0)

        acc = lax.fori_loop(
            0, rows // step_rows, body, jnp.zeros((8, width), F32), unroll=4
        )
        total = jnp.sum(acc, axis=0, keepdims=True)
        for g in range(groups):
            col_buf[c, g : g + 1, :] = total[:, g * LANES : (g + 1) * LANES]

    def send_cols(d):
        peer = lax.rem(me + d, n)
        return pltpu.make_async_remote_copy(
            src_ref=col_buf.at[peer], dst_ref=col_recv.at[d],
            send_sem=col_send.at[d], recv_sem=col_recv_sem.at[d],
            device_id={"fsdp": peer}, device_id_type=MESH,
        )

    for d in range(1, n):
        send_cols(d).start()

    row_line = jnp.sum(jnp.transpose(row_acc[...]), axis=0, keepdims=True)
    row_buf[...] = jnp.zeros_like(row_buf)
    for g in range(row_groups):
        row_buf[g : g + 1, :] = row_line[:, g * LANES : (g + 1) * LANES]
    send_rows = pltpu.make_async_remote_copy(
        src_ref=row_buf, dst_ref=row_recv, send_sem=row_sems.at[0], recv_sem=row_sems.at[1],
        device_id={"tp": 1 - core}, device_id_type=MESH,
    )
    send_rows.start()

    def biggest(c, m):
        wload(c).wait()

        def inner(r, m):
            x = jnp.abs(weight_buf[c, pl.ds(pl.multiple_of(r * 64, 64), 64), :])
            for g in range(groups):
                for k in range(4):
                    m = jnp.maximum(m, x[k * 16 : k * 16 + 16, g * LANES : (g + 1) * LANES])
            return m

        return lax.fori_loop(0, rows // 64, inner, m)

    weight_max = lax.fori_loop(0, CHUNKS, biggest, jnp.zeros((16, LANES), BF16))
    weight_max = jnp.max(weight_max.astype(F32), axis=(0, 1), keepdims=True)

    send_rows.wait()
    row_total = row_buf[...] + row_recv[...]
    new_rows = 0.8 * row_moment_ref[...] + 0.2 * (row_total[:row_groups] / ff + 1e-30)
    rows_ref[...] = new_rows
    rows_summed = jnp.sum(new_rows, axis=(0, 1), keepdims=True)
    rows_least = jnp.min(new_rows, axis=(0, 1), keepdims=True)

    col_total = col_buf[me]
    for d in range(1, n):
        send_cols(d).wait()
        col_total = col_total + col_recv[d]
    msg[0:chunk] = col_total
    msg[chunk : chunk + 8] = jnp.zeros((8, LANES), F32)
    msg[chunk : chunk + 1] = jnp.broadcast_to(rows_summed, (1, LANES))
    msg[chunk + 1 : chunk + 2] = jnp.broadcast_to(rows_least, (1, LANES))
    msg[chunk + 2 : chunk + 3] = jnp.broadcast_to(weight_max, (1, LANES))

    def send_msg(d):
        return pltpu.make_async_remote_copy(
            src_ref=msg, dst_ref=all_buf.at[me],
            send_sem=msg_send.at[d], recv_sem=msg_recv.at[d],
            device_id={"fsdp": lax.rem(me + d, n)}, device_id_type=MESH,
        )

    for d in range(1, n):
        send_msg(d).start()
    all_buf[me] = msg[...]

    for d in range(1, n):
        send_normed(d).wait()
    give = pltpu.make_async_remote_copy(
        src_ref=norm_got.at[core], dst_ref=norm_got.at[core],
        send_sem=pass_sems.at[0], recv_sem=pass_sems.at[1],
        device_id={"tp": 1 - core}, device_id_type=MESH,
    )
    give.start()
    factor = 0.01 * lax.rsqrt(new_rows)
    for g in range(row_groups):
        line = jnp.broadcast_to(factor[g : g + 1, :], (LANES, LANES))
        row_factor[g * LANES : (g + 1) * LANES, :] = jnp.transpose(line)

    for d in range(1, n):
        send_msg(d).wait()
    summed = all_buf[0, chunk : chunk + 1, :]
    least = all_buf[0, chunk + 1 : chunk + 2, :]
    heaviest = all_buf[0, chunk + 2 : chunk + 3, :]
    for o in range(1, n):
        summed = summed + all_buf[o, chunk : chunk + 1, :]
        least = jnp.minimum(least, all_buf[o, chunk + 1 : chunk + 2, :])
        heaviest = jnp.maximum(heaviest, all_buf[o, chunk + 2 : chunk + 3, :])
    row_scale = summed / d_model
    root = jnp.sqrt(row_scale)
    ratio = jnp.zeros((1, LANES), F32)
    for o in range(n):
        here = slice(o * chunk, (o + 1) * chunk)
        sums = all_buf[o, 0:chunk, :]
        new_columns = 0.8 * col_moment_ref[here, :] + 0.2 * (sums / d_model + 1e-30)
        cols_ref[here, :] = new_columns
        scaled = lax.rsqrt(new_columns) * root
        col_factor[o] = scaled
        ratio = jnp.maximum(ratio, jnp.max(sums / new_columns, axis=0, keepdims=True))
    ratio = jnp.max(ratio, axis=1, keepdims=True)

    column_norm = d_model**0.5 * heaviest + 0.01 * jnp.sqrt(row_scale / least * ratio)
    bound = (1.02 * GAIN_MAX * d_model**0.5 * column_norm + 1e-25)[:, 0:1]
    scale = 8000.0 / bound
    unscale = bound / 8000.0
    give.wait()

    place = jnp.where(lax.rem(me, 2) == 0, me // 2, n - 1 - me // 2)

    def device_at(q):
        q = lax.rem(q + n, n)
        return jnp.where(q < n // 2, 2 * q, 2 * (n - 1 - q) + 1)

    neighbours = (device_at(place + 1), device_at(place - 1))

    def copy(way, step, c):
        return pltpu.make_async_remote_copy(
            src_ref=sent.at[way, step, c],
            dst_ref=got.at[way, step, c],
            send_sem=send_sem.at[way, step, c],
            recv_sem=recv_sem.at[way, step, c],
            device_id={"fsdp": neighbours[way]},
            device_id_type=MESH,
        )

    def pass_on(way, step, c, first):
        far = steps - step
        dest = device_at(place + far) if way == 0 else device_at(place - far)
        total = part[c, dest]
        if not first:
            copy(way, step - 1, c).wait_recv()
            total = total + decode(got[way, step - 1, c], unscale)
        sent[way, step, c] = encode(total * scale)
        copy(way, step, c).start()

    @pl.loop(0, CHUNKS // 2)
    def _(pair):
        for way in range(2):
            c = 2 * pair + way

            @pl.loop(0, row_groups)
            def _(r):
                block = pl.ds(pl.multiple_of(r * LANES, LANES), LANES)
                for g in range(groups):
                    at = slice(g * LANES, (g + 1) * LANES)
                    change = (
                        grad_buf[c, block, at].astype(F32)
                        * row_factor[block, :]
                        * col_factor[c, g : g + 1, :]
                    )
                    weight_buf[c, block, at] = (
                        weight_buf[c, block, at].astype(F32) - change
                    ).astype(BF16)

            store(c).start()
            product = jnp.dot(
                norm_got[0].reshape(n * tokens, half), weight_buf[c, :half, :],
                preferred_element_type=F32,
            ) + jnp.dot(
                norm_got[1].reshape(n * tokens, half), weight_buf[c, half:, :],
                preferred_element_type=F32,
            )
            part[c] = product.reshape(n, tokens, width)
            pass_on(way, 0, c, True)
            pass_on(1 - way, 1, c, True)

    @pl.loop(0, CHUNKS // 2)
    def _(pair):
        for way in range(2):
            pass_on(way, 1, 2 * pair + way, False)

    for step in range(2, steps):

        @pl.loop(0, CHUNKS)
        def _(c):
            for way in range(2):
                pass_on(way, step, c, False)

    @pl.loop(0, CHUNKS)
    def _(c):
        total = part[c, me]
        for way in range(2):
            copy(way, steps - 1, c).wait_recv()
            total = total + decode(got[way, steps - 1, c], unscale)
        up_ref[:, columns(c)] = total.astype(BF16)

    @pl.loop(0, CHUNKS // 2)
    def _(pair):
        for way in range(2):
            store(2 * pair + way).wait()
            copy(way, 0, 2 * pair + way).wait_send()
            for step in range(1, steps):
                for parity in range(2):
                    copy(way, step, 2 * pair + parity).wait_send()


def kernels_fit(n, tp, rows, cols, tokens):
    held = 2 * rows * cols * 2 + n * tokens * cols * (4 + 2 + 2) + tokens * cols * 2
    held += 4 * n * tokens * rows * 2 + 2 * tokens * n * rows * 4
    return (
        tp == 2
        and n >= 4
        and n == CHUNKS
        and rows % (2 * LANES) == 0
        and rows // LANES <= 8
        and cols % (8 * LANES * n) == 0
        and tokens % 16 == 0
        and held <= VMEM_BUDGET - (4 << 20)
    )


def with_kernels(n, ff, d_model, weight, grad, row_moment, col_moment, states, gain, gate):
    rows, cols = grad.shape
    tokens = states.shape[0]
    chunk = cols // n // LANES
    half = rows // 2
    width = cols // CHUNKS
    slots = (2, n // 2, CHUNKS)
    vmem = pl.BlockSpec(memory_space=pltpu.VMEM)
    hbm = pl.BlockSpec(memory_space=pl.ANY)
    shape = jax.ShapeDtypeStruct
    dma = pltpu.SemaphoreType.DMA
    new_weight, new_rows, new_columns, up_values = pl.pallas_call(
        functools.partial(step_kernel, n, ff, d_model),
        out_shape=(
            shape((rows, cols), BF16),
            shape((rows // LANES, LANES), F32),
            shape((cols // LANES, LANES), F32),
            shape((tokens, cols), BF16),
        ),
        in_specs=[hbm, hbm, vmem, vmem, vmem, vmem],
        out_specs=(hbm, vmem, vmem, vmem),
        scratch_shapes=[
            pltpu.VMEM((CHUNKS, rows, width), BF16),
            pltpu.VMEM((CHUNKS, rows, width), BF16),
            pltpu.VMEM((rows, LANES), F32),
            pltpu.VMEM((8, LANES), F32),
            pltpu.VMEM((8, LANES), F32),
            pltpu.VMEM((n, chunk, LANES), F32),
            pltpu.VMEM((n, chunk, LANES), F32),
            pltpu.VMEM((chunk + 8, LANES), F32),
            pltpu.VMEM((n, chunk + 8, LANES), F32),
            pltpu.VMEM((2, n, tokens, half), BF16),
            pltpu.VMEM((2, n, tokens, half), BF16),
            pltpu.VMEM((rows, LANES), F32),
            pltpu.VMEM((CHUNKS, width // LANES, LANES), F32),
            pltpu.VMEM((CHUNKS, n, tokens, width), F32),
            pltpu.VMEM((*slots, tokens, width), BF16),
            pltpu.VMEM((*slots, tokens, width), BF16),
            dma((CHUNKS,)), dma((CHUNKS,)), dma((CHUNKS,)), dma((2,)), dma((n,)), dma((n,)),
            dma((n,)), dma((n,)), dma((n,)), dma((n,)), dma((2,)), dma(slots), dma(slots),
        ],
        compiler_params=pltpu.CompilerParams(
            collective_id=0, has_side_effects=True, vmem_limit_bytes=VMEM_BUDGET
        ),
        name="whole_step",
    )(
        grad, weight, row_moment.reshape(rows // LANES, LANES),
        col_moment.reshape(cols // LANES, LANES), states, gain.reshape(1, -1),
    )
    hidden = (jax.nn.silu(gate.astype(F32)) * up_values.astype(F32)).astype(BF16)
    return new_weight, new_rows.reshape(-1), new_columns.reshape(-1), hidden


def with_collectives(ff, d_model, weight, grad, row_moment, col_moment, states, gain, gate):
    gradient = grad.astype(F32)
    squares = gradient * gradient + 1e-30
    row_total = lax.psum(jnp.sum(squares, axis=1), "tp")
    new_rows = 0.8 * row_moment + 0.2 * (row_total / ff)
    col_total, rows_summed = lax.psum((jnp.sum(squares, axis=0), jnp.sum(new_rows)), "fsdp")
    new_columns = 0.8 * col_moment + 0.2 * (col_total / d_model)
    row_scale = rows_summed / d_model
    change = gradient / jnp.sqrt(new_rows[:, None] * new_columns[None, :] / row_scale)
    new_weight = (weight.astype(F32) - 0.01 * change).astype(BF16)
    values = states.astype(F32)
    normed = (
        values
        * lax.rsqrt(jnp.mean(values * values, axis=1, keepdims=True) + 1e-06)
        * gain.astype(F32)
    ).astype(BF16)
    column_block = lax.all_to_all(new_weight, "fsdp", split_axis=1, concat_axis=0, tiled=True)
    up_block = jnp.dot(
        lax.all_gather(normed, "fsdp", axis=0, tiled=True),
        column_block,
        preferred_element_type=F32,
    ).astype(BF16)
    up_values = lax.all_to_all(up_block, "fsdp", split_axis=0, concat_axis=1, tiled=True)
    hidden = (jax.nn.silu(gate.astype(F32)) * up_values.astype(F32)).astype(BF16)
    return new_weight, new_rows, new_columns, hidden


def solution(mesh):
    n, tp = mesh.shape["fsdp"], mesh.shape["tp"]

    def on_device(weight, grad, row_moment, col_moment, states, gain, gate):
        rows, cols = weight.shape
        ff, d_model = cols * tp, rows * n
        arrays = (weight, grad, row_moment, col_moment, states, gain, gate)
        if kernels_fit(n, tp, rows, cols, states.shape[0]):
            return with_kernels(n, ff, d_model, *arrays)
        return with_collectives(ff, d_model, *arrays)

    return jax.shard_map(
        on_device,
        mesh=mesh,
        in_specs=(
            P(("job", "fsdp"), "tp"),
            P(("job", "fsdp"), "tp"),
            P(("job", "fsdp")),
            P(("job", "tp")),
            P(("job", "fsdp"), None),
            P("job"),
            P(("job", "fsdp"), "tp"),
        ),
        out_specs=(
            P(("job", "fsdp"), "tp"),
            P(("job", "fsdp")),
            P(("job", "tp")),
            P(("job", "fsdp"), "tp"),
        ),
        check_vma=False,
    )
```

```python
import functools
import jax
import jax.numpy as jnp
from jax import lax
from jax.experimental import pallas as pl
from jax.experimental.pallas import tpu as pltpu
from jax.sharding import PartitionSpec as P

MESH = pl.DeviceIdType.MESH
F32 = jnp.float32
BF16 = jnp.bfloat16
LANES = 128
HALVES = 2
POWER = 9
VMEM_BUDGET = 56 * 1024 * 1024
GAIN_MAX = 1.8984375


def encode(v):
    square = v * v
    fourth = square * square
    return (fourth * fourth * v).astype(BF16)


def decode(code, unscale):
    c = code.astype(F32)
    size = jnp.exp2(jnp.log2(jnp.abs(c)) * (1.0 / POWER)) * unscale
    return jnp.where(c < 0, -size, size)


def step_kernel(
    n, ff, d_model,
    grad_ref, weight_ref, row_moment_ref, col_moment_ref, states_ref, gain_ref,
    new_weight_ref, rows_ref, cols_ref, up_ref,
    grad_buf, weight_buf, row_acc, row_buf, row_recv, col_buf, col_recv, msg, all_buf,
    norm_buf, norm_got, row_factor, col_factor, part, sent, got,
    load_sem, wload_sem, store_sem, row_sems, col_send, col_recv_sem, msg_send, msg_recv,
    norm_send, norm_recv, pass_sems, send_sem, recv_sem,
):
    me = lax.axis_index("fsdp")
    core = lax.axis_index("tp")
    rows, cols = grad_ref.shape
    chunks = HALVES * n
    width = cols // chunks
    groups = width // LANES
    chunk = cols // n // LANES
    row_groups = rows // LANES
    tokens = states_ref.shape[0]
    half = rows // 2
    steps = n // 2

    def columns(c):
        return pl.ds(pl.multiple_of(c * width, LANES), width)

    def load(c):
        return pltpu.make_async_copy(grad_ref.at[:, columns(c)], grad_buf.at[c], load_sem.at[c])

    def wload(c):
        return pltpu.make_async_copy(
            weight_ref.at[:, columns(c)], weight_buf.at[c], wload_sem.at[c]
        )

    def store(c):
        return pltpu.make_async_copy(
            weight_buf.at[c], new_weight_ref.at[:, columns(c)], store_sem.at[c]
        )

    for c in range(chunks):
        load(c).start()
    for c in range(chunks):
        wload(c).start()

    barrier = pltpu.get_barrier_semaphore()
    for d in range(1, n):
        pl.semaphore_signal(
            barrier, inc=1, device_id={"fsdp": lax.rem(me + d, n)}, device_id_type=MESH
        )
    pl.semaphore_signal(barrier, inc=1, device_id={"tp": 1 - core}, device_id_type=MESH)

    values = states_ref[...].astype(F32)
    inverse = lax.rsqrt(jnp.mean(values * values, axis=1, keepdims=True) + 1e-06)
    gain = gain_ref[...].astype(F32)
    for g in range(d_model // LANES):
        at = g * LANES
        p, h, inside = at // rows, at % rows // half, at % half
        norm_buf[h, p, :, inside : inside + LANES] = (
            values[:, at : at + LANES] * inverse * gain[g : g + 1, :]
        ).astype(BF16)
    pl.semaphore_wait(barrier, n)

    def send_normed(d):
        peer = lax.rem(me + d, n)
        return pltpu.make_async_remote_copy(
            src_ref=norm_buf.at[core, peer],
            dst_ref=norm_got.at[core, me],
            send_sem=norm_send.at[d],
            recv_sem=norm_recv.at[d],
            device_id={"fsdp": peer},
            device_id_type=MESH,
        )

    for d in range(1, n):
        send_normed(d).start()
    norm_got[core, me] = norm_buf[core, me]

    row_acc[...] = jnp.zeros_like(row_acc)
    step_rows = 32

    @pl.loop(0, n)
    def _(p):
        for k in range(HALVES):
            load(HALVES * p + k).wait()

        def body(r, accs):
            at = pl.multiple_of(r * step_rows, step_rows)
            lane = row_acc[pl.ds(at, step_rows), :]
            out = []
            for k in range(HALVES):
                x = grad_buf[HALVES * p + k, pl.ds(at, step_rows), :].astype(F32)
                sq = x * x
                for g in range(groups):
                    lane = lane + sq[:, g * LANES : (g + 1) * LANES]
                out.append(accs[k] + jnp.sum(sq.reshape(step_rows // 8, 8, width), axis=0))
            row_acc[pl.ds(at, step_rows), :] = lane
            return tuple(out)

        accs = lax.fori_loop(
            0, rows // step_rows, body, (jnp.zeros((8, width), F32),) * HALVES, unroll=4
        )
        for k in range(HALVES):
            total = jnp.sum(accs[k], axis=0, keepdims=True)
            for g in range(groups):
                line = k * groups + g
                col_buf[p, line : line + 1, :] = total[:, g * LANES : (g + 1) * LANES]

    def send_cols(d):
        peer = lax.rem(me + d, n)
        return pltpu.make_async_remote_copy(
            src_ref=col_buf.at[peer], dst_ref=col_recv.at[d],
            send_sem=col_send.at[d], recv_sem=col_recv_sem.at[d],
            device_id={"fsdp": peer}, device_id_type=MESH,
        )

    for d in range(1, n):
        send_cols(d).start()

    row_line = jnp.sum(jnp.transpose(row_acc[...]), axis=0, keepdims=True)
    row_buf[...] = jnp.zeros_like(row_buf)
    for g in range(row_groups):
        row_buf[g : g + 1, :] = row_line[:, g * LANES : (g + 1) * LANES]
    send_rows = pltpu.make_async_remote_copy(
        src_ref=row_buf, dst_ref=row_recv, send_sem=row_sems.at[0], recv_sem=row_sems.at[1],
        device_id={"tp": 1 - core}, device_id_type=MESH,
    )
    send_rows.start()

    def biggest(c, m):
        wload(c).wait()

        def inner(r, m):
            x = jnp.abs(weight_buf[c, pl.ds(pl.multiple_of(r * 64, 64), 64), :])
            for g in range(groups):
                for k in range(4):
                    m = jnp.maximum(m, x[k * 16 : k * 16 + 16, g * LANES : (g + 1) * LANES])
            return m

        return lax.fori_loop(0, rows // 64, inner, m)

    weight_max = lax.fori_loop(0, chunks, biggest, jnp.zeros((16, LANES), BF16))
    weight_max = jnp.max(weight_max.astype(F32), axis=(0, 1), keepdims=True)

    send_rows.wait()
    row_total = row_buf[...] + row_recv[...]
    new_rows = 0.8 * row_moment_ref[...] + 0.2 * (row_total[:row_groups] / ff + 1e-30)
    rows_ref[...] = new_rows
    rows_summed = jnp.sum(new_rows, axis=(0, 1), keepdims=True)
    rows_least = jnp.min(new_rows, axis=(0, 1), keepdims=True)

    col_total = col_buf[me]
    for d in range(1, n):
        send_cols(d).wait()
        col_total = col_total + col_recv[d]
    msg[0:chunk] = col_total
    msg[chunk : chunk + 8] = jnp.zeros((8, LANES), F32)
    msg[chunk : chunk + 1] = jnp.broadcast_to(rows_summed, (1, LANES))
    msg[chunk + 1 : chunk + 2] = jnp.broadcast_to(rows_least, (1, LANES))
    msg[chunk + 2 : chunk + 3] = jnp.broadcast_to(weight_max, (1, LANES))

    def send_msg(d):
        return pltpu.make_async_remote_copy(
            src_ref=msg, dst_ref=all_buf.at[me],
            send_sem=msg_send.at[d], recv_sem=msg_recv.at[d],
            device_id={"fsdp": lax.rem(me + d, n)}, device_id_type=MESH,
        )

    for d in range(1, n):
        send_msg(d).start()
    all_buf[me] = msg[...]

    for d in range(1, n):
        send_normed(d).wait()
    give = pltpu.make_async_remote_copy(
        src_ref=norm_got.at[core], dst_ref=norm_got.at[core],
        send_sem=pass_sems.at[0], recv_sem=pass_sems.at[1],
        device_id={"tp": 1 - core}, device_id_type=MESH,
    )
    give.start()
    factor = 0.01 * lax.rsqrt(new_rows)
    for g in range(row_groups):
        line = jnp.broadcast_to(factor[g : g + 1, :], (LANES, LANES))
        row_factor[g * LANES : (g + 1) * LANES, :] = jnp.transpose(line)

    for d in range(1, n):
        send_msg(d).wait()
    summed = all_buf[0, chunk : chunk + 1, :]
    least = all_buf[0, chunk + 1 : chunk + 2, :]
    heaviest = all_buf[0, chunk + 2 : chunk + 3, :]
    for o in range(1, n):
        summed = summed + all_buf[o, chunk : chunk + 1, :]
        least = jnp.minimum(least, all_buf[o, chunk + 1 : chunk + 2, :])
        heaviest = jnp.maximum(heaviest, all_buf[o, chunk + 2 : chunk + 3, :])
    row_scale = summed / d_model
    root = jnp.sqrt(row_scale)
    ratio = jnp.zeros((1, LANES), F32)
    for o in range(n):
        here = slice(o * chunk, (o + 1) * chunk)
        sums = all_buf[o, 0:chunk, :]
        new_columns = 0.8 * col_moment_ref[here, :] + 0.2 * (sums / d_model + 1e-30)
        cols_ref[here, :] = new_columns
        scaled = lax.rsqrt(new_columns) * root
        col_factor[o] = scaled
        ratio = jnp.maximum(ratio, jnp.max(sums / new_columns, axis=0, keepdims=True))
    ratio = jnp.max(ratio, axis=1, keepdims=True)

    column_norm = d_model**0.5 * heaviest + 0.01 * jnp.sqrt(row_scale / least * ratio)
    bound = (1.02 * GAIN_MAX * d_model**0.5 * column_norm + 1e-25)[:, 0:1]
    scale = 8000.0 / bound
    unscale = bound / 8000.0
    give.wait()

    place = jnp.where(lax.rem(me, 2) == 0, me // 2, n - 1 - me // 2)

    def device_at(q):
        q = lax.rem(q + n, n)
        return jnp.where(q < n // 2, 2 * q, 2 * (n - 1 - q) + 1)

    neighbours = (device_at(place + 1), device_at(place - 1))

    def copy(way, step, c):
        return pltpu.make_async_remote_copy(
            src_ref=sent.at[way, step, c],
            dst_ref=got.at[way, step, c],
            send_sem=send_sem.at[way, step, c],
            recv_sem=recv_sem.at[way, step, c],
            device_id={"fsdp": neighbours[way]},
            device_id_type=MESH,
        )

    def pass_on(way, step, c, first):
        far = steps - step
        dest = device_at(place + far) if way == 0 else device_at(place - far)
        total = part[c, dest]
        if not first:
            copy(way, step - 1, c).wait_recv()
            total = total + decode(got[way, step - 1, c], unscale)
        sent[way, step, c] = encode(total * scale)
        copy(way, step, c).start()

    @pl.loop(0, n)
    def _(pair):
        for way in range(2):
            c = 2 * pair + way

            @pl.loop(0, row_groups)
            def _(r):
                block = pl.ds(pl.multiple_of(r * LANES, LANES), LANES)
                for g in range(groups):
                    at = slice(g * LANES, (g + 1) * LANES)
                    change = (
                        grad_buf[c, block, at].astype(F32)
                        * row_factor[block, :]
                        * col_factor[pair, way * groups + g : way * groups + g + 1, :]
                    )
                    weight_buf[c, block, at] = (
                        weight_buf[c, block, at].astype(F32) - change
                    ).astype(BF16)

            store(c).start()
            product = jnp.dot(
                norm_got[0].reshape(n * tokens, half), weight_buf[c, :half, :],
                preferred_element_type=F32,
            ) + jnp.dot(
                norm_got[1].reshape(n * tokens, half), weight_buf[c, half:, :],
                preferred_element_type=F32,
            )
            part[c] = product.reshape(n, tokens, width)
            pass_on(way, 0, c, True)
            pass_on(1 - way, 1, c, True)

    @pl.loop(0, n)
    def _(pair):
        for way in range(2):
            pass_on(way, 1, 2 * pair + way, False)

    for step in range(2, steps):

        @pl.loop(0, chunks)
        def _(c):
            for way in range(2):
                pass_on(way, step, c, False)

    @pl.loop(0, chunks)
    def _(c):
        total = part[c, me]
        for way in range(2):
            copy(way, steps - 1, c).wait_recv()
            total = total + decode(got[way, steps - 1, c], unscale)
        up_ref[:, columns(c)] = total.astype(BF16)

    @pl.loop(0, n)
    def _(pair):
        for way in range(2):
            store(2 * pair + way).wait()
            copy(way, 0, 2 * pair + way).wait_send()
            for step in range(1, steps):
                for parity in range(2):
                    copy(way, step, 2 * pair + parity).wait_send()


def finish_kernel(
    made_ref, gate_ref, up_ref, rows_in, cols_in, weight_ref, hidden_ref, rows_out, cols_out,
    buf, in_sem, out_sem,
):
    pieces, height = buf.shape[0], buf.shape[1]

    def fetch(p):
        at = pl.ds(p * height, height)
        return pltpu.make_async_copy(made_ref.at[at, :], buf.at[p], in_sem.at[p])

    def store(p):
        at = pl.ds(p * height, height)
        return pltpu.make_async_copy(buf.at[p], weight_ref.at[at, :], out_sem.at[p])

    for p in range(pieces):
        fetch(p).start()
    rows_out[...] = rows_in[...]
    cols_out[...] = cols_in[...]
    each = gate_ref.shape[1] // pieces
    for p in range(pieces):
        at = slice(p * each, (p + 1) * each)
        gate = gate_ref[:, at].astype(F32)
        silu = gate / (1.0 + jnp.exp(-gate))
        hidden_ref[:, at] = (silu * up_ref[:, at].astype(F32)).astype(BF16)
        fetch(p).wait()
        store(p).start()
    for p in range(pieces):
        store(p).wait()


def finish(made, gate, up_values, new_rows, new_columns):
    rows, cols = made.shape
    pieces = 16
    vmem = pl.BlockSpec(memory_space=pltpu.VMEM)
    hbm = pl.BlockSpec(memory_space=pl.ANY)
    return pl.pallas_call(
        finish_kernel,
        out_shape=(
            jax.ShapeDtypeStruct(made.shape, BF16),
            jax.ShapeDtypeStruct(gate.shape, BF16),
            jax.ShapeDtypeStruct(new_rows.shape, F32),
            jax.ShapeDtypeStruct(new_columns.shape, F32),
        ),
        in_specs=[hbm, vmem, vmem, vmem, vmem],
        out_specs=(hbm, vmem, vmem, vmem),
        scratch_shapes=[
            pltpu.VMEM((pieces, rows // pieces, cols), BF16),
            pltpu.SemaphoreType.DMA((pieces,)),
            pltpu.SemaphoreType.DMA((pieces,)),
        ],
        compiler_params=pltpu.CompilerParams(vmem_limit_bytes=VMEM_BUDGET),
        name="finish",
    )(made, gate, up_values, new_rows, new_columns)


def kernels_fit(n, tp, rows, cols, tokens):
    held = 2 * rows * cols * 2 + n * tokens * cols * (4 + 2 + 2) + tokens * cols * 2
    held += 4 * n * tokens * rows * 2 + 2 * tokens * n * rows * 4
    return (
        tp == 2
        and n >= 4
        and rows % (2 * LANES) == 0
        and rows // LANES <= 8
        and cols % (8 * LANES * n) == 0
        and cols % (HALVES * LANES * n) == 0
        and tokens % 16 == 0
        and held <= VMEM_BUDGET - (4 << 20)
    )


def with_kernels(n, ff, d_model, weight, grad, row_moment, col_moment, states, gain, gate):
    rows, cols = grad.shape
    tokens = states.shape[0]
    chunk = cols // n // LANES
    half = rows // 2
    chunks = HALVES * n
    width = cols // chunks
    slots = (2, n // 2, chunks)
    vmem = pl.BlockSpec(memory_space=pltpu.VMEM)
    hbm = pl.BlockSpec(memory_space=pl.ANY)
    shape = jax.ShapeDtypeStruct
    dma = pltpu.SemaphoreType.DMA
    new_weight, new_rows, new_columns, up_values = pl.pallas_call(
        functools.partial(step_kernel, n, ff, d_model),
        out_shape=(
            shape((rows, cols), BF16),
            shape((rows // LANES, LANES), F32),
            shape((cols // LANES, LANES), F32),
            shape((tokens, cols), BF16),
        ),
        in_specs=[hbm, hbm, vmem, vmem, vmem, vmem],
        out_specs=(hbm, vmem, vmem, vmem),
        scratch_shapes=[
            pltpu.VMEM((chunks, rows, width), BF16),
            pltpu.VMEM((chunks, rows, width), BF16),
            pltpu.VMEM((rows, LANES), F32),
            pltpu.VMEM((8, LANES), F32),
            pltpu.VMEM((8, LANES), F32),
            pltpu.VMEM((n, chunk, LANES), F32),
            pltpu.VMEM((n, chunk, LANES), F32),
            pltpu.VMEM((chunk + 8, LANES), F32),
            pltpu.VMEM((n, chunk + 8, LANES), F32),
            pltpu.VMEM((2, n, tokens, half), BF16),
            pltpu.VMEM((2, n, tokens, half), BF16),
            pltpu.VMEM((rows, LANES), F32),
            pltpu.VMEM((n, chunk, LANES), F32),
            pltpu.VMEM((chunks, n, tokens, width), F32),
            pltpu.VMEM((*slots, tokens, width), BF16),
            pltpu.VMEM((*slots, tokens, width), BF16),
            dma((chunks,)), dma((chunks,)), dma((chunks,)), dma((2,)), dma((n,)), dma((n,)),
            dma((n,)), dma((n,)), dma((n,)), dma((n,)), dma((2,)), dma(slots), dma(slots),
        ],
        compiler_params=pltpu.CompilerParams(
            collective_id=0, has_side_effects=True, vmem_limit_bytes=VMEM_BUDGET
        ),
        name="whole_step",
    )(
        grad, weight, row_moment.reshape(rows // LANES, LANES),
        col_moment.reshape(cols // LANES, LANES), states, gain.reshape(-1, LANES),
    )
    new_weight, hidden, new_rows, new_columns = finish(
        new_weight, gate, up_values, new_rows, new_columns
    )
    return new_weight, new_rows.reshape(-1), new_columns.reshape(-1), hidden


def with_collectives(ff, d_model, weight, grad, row_moment, col_moment, states, gain, gate):
    gradient = grad.astype(F32)
    squares = gradient * gradient + 1e-30
    row_total = lax.psum(jnp.sum(squares, axis=1), "tp")
    new_rows = 0.8 * row_moment + 0.2 * (row_total / ff)
    col_total, rows_summed = lax.psum((jnp.sum(squares, axis=0), jnp.sum(new_rows)), "fsdp")
    new_columns = 0.8 * col_moment + 0.2 * (col_total / d_model)
    row_scale = rows_summed / d_model
    change = gradient / jnp.sqrt(new_rows[:, None] * new_columns[None, :] / row_scale)
    new_weight = (weight.astype(F32) - 0.01 * change).astype(BF16)
    values = states.astype(F32)
    normed = (
        values
        * lax.rsqrt(jnp.mean(values * values, axis=1, keepdims=True) + 1e-06)
        * gain.astype(F32)
    ).astype(BF16)
    column_block = lax.all_to_all(new_weight, "fsdp", split_axis=1, concat_axis=0, tiled=True)
    up_block = jnp.dot(
        lax.all_gather(normed, "fsdp", axis=0, tiled=True),
        column_block,
        preferred_element_type=F32,
    ).astype(BF16)
    up_values = lax.all_to_all(up_block, "fsdp", split_axis=0, concat_axis=1, tiled=True)
    hidden = (jax.nn.silu(gate.astype(F32)) * up_values.astype(F32)).astype(BF16)
    return new_weight, new_rows, new_columns, hidden


def solution(mesh):
    n, tp = mesh.shape["fsdp"], mesh.shape["tp"]

    def on_device(weight, grad, row_moment, col_moment, states, gain, gate):
        rows, cols = weight.shape
        ff, d_model = cols * tp, rows * n
        arrays = (weight, grad, row_moment, col_moment, states, gain, gate)
        if kernels_fit(n, tp, rows, cols, states.shape[0]):
            return with_kernels(n, ff, d_model, *arrays)
        return with_collectives(ff, d_model, *arrays)

    return jax.shard_map(
        on_device,
        mesh=mesh,
        in_specs=(
            P(("job", "fsdp"), "tp"),
            P(("job", "fsdp"), "tp"),
            P(("job", "fsdp")),
            P(("job", "tp")),
            P(("job", "fsdp"), None),
            P("job"),
            P(("job", "fsdp"), "tp"),
        ),
        out_specs=(
            P(("job", "fsdp"), "tp"),
            P(("job", "fsdp")),
            P(("job", "tp")),
            P(("job", "fsdp"), "tp"),
        ),
        check_vma=False,
    )
```

```python
import functools
import jax
import jax.numpy as jnp
from jax import lax
from jax.experimental import pallas as pl
from jax.experimental.pallas import tpu as pltpu
from jax.sharding import PartitionSpec as P

MESH = pl.DeviceIdType.MESH
F32 = jnp.float32
BF16 = jnp.bfloat16
LANES = 128
HALVES = 2
POWER = 9
VMEM_BUDGET = 56 * 1024 * 1024
GAIN_MAX = 1.8984375


def encode(v):
    square = v * v
    fourth = square * square
    return (fourth * fourth * v).astype(BF16)


def decode(code, unscale):
    c = code.astype(F32)
    size = jnp.exp2(jnp.log2(jnp.abs(c)) * (1.0 / POWER)) * unscale
    return jnp.where(c < 0, -size, size)


def step_kernel(
    n, ff, d_model,
    grad_ref, weight_ref, row_moment_ref, col_moment_ref, states_ref, gain_ref,
    new_weight_ref, rows_ref, cols_ref, up_ref,
    grad_buf, weight_buf, row_acc, row_buf, row_recv, col_buf, col_recv, msg, all_buf,
    norm_buf, norm_got, row_factor, col_factor, part, sent, got,
    load_sem, wload_sem, store_sem, row_sems, col_send, col_recv_sem, msg_send, msg_recv,
    norm_send, norm_recv, pass_sems, send_sem, recv_sem,
):
    me = lax.axis_index("fsdp")
    core = lax.axis_index("tp")
    rows, cols = grad_ref.shape
    chunks = HALVES * n
    width = cols // chunks
    groups = width // LANES
    chunk = cols // n // LANES
    row_groups = rows // LANES
    tokens = states_ref.shape[0]
    half = rows // 2
    steps = n // 2

    def columns(c):
        return pl.ds(pl.multiple_of(c * width, LANES), width)

    def load(c):
        return pltpu.make_async_copy(grad_ref.at[:, columns(c)], grad_buf.at[c], load_sem.at[c])

    def wload(c):
        return pltpu.make_async_copy(
            weight_ref.at[:, columns(c)], weight_buf.at[c], wload_sem.at[c]
        )

    def store(c):
        return pltpu.make_async_copy(
            weight_buf.at[c], new_weight_ref.at[:, columns(c)], store_sem.at[c]
        )

    for c in range(chunks):
        load(c).start()
    for c in range(chunks):
        wload(c).start()

    barrier = pltpu.get_barrier_semaphore()
    for d in range(1, n):
        pl.semaphore_signal(
            barrier, inc=1, device_id={"fsdp": lax.rem(me + d, n)}, device_id_type=MESH
        )
    pl.semaphore_signal(barrier, inc=1, device_id={"tp": 1 - core}, device_id_type=MESH)

    values = states_ref[...].astype(F32)
    inverse = lax.rsqrt(jnp.mean(values * values, axis=1, keepdims=True) + 1e-06)
    gain = gain_ref[...].astype(F32)
    for g in range(d_model // LANES):
        at = g * LANES
        p, h, inside = at // rows, at % rows // half, at % half
        norm_buf[h, p, :, inside : inside + LANES] = (
            values[:, at : at + LANES] * inverse * gain[g : g + 1, :]
        ).astype(BF16)
    pl.semaphore_wait(barrier, n)

    def send_normed(d):
        peer = lax.rem(me + d, n)
        return pltpu.make_async_remote_copy(
            src_ref=norm_buf.at[core, peer],
            dst_ref=norm_got.at[core, me],
            send_sem=norm_send.at[d],
            recv_sem=norm_recv.at[d],
            device_id={"fsdp": peer},
            device_id_type=MESH,
        )

    for d in range(1, n):
        send_normed(d).start()
    norm_got[core, me] = norm_buf[core, me]

    row_acc[...] = jnp.zeros_like(row_acc)
    step_rows = 32

    @pl.loop(0, n)
    def _(p):
        for k in range(HALVES):
            load(HALVES * p + k).wait()

        def body(r, accs):
            at = pl.multiple_of(r * step_rows, step_rows)
            lane = row_acc[pl.ds(at, step_rows), :]
            out = []
            for k in range(HALVES):
                x = grad_buf[HALVES * p + k, pl.ds(at, step_rows), :].astype(F32)
                sq = x * x
                for g in range(groups):
                    lane = lane + sq[:, g * LANES : (g + 1) * LANES]
                out.append(accs[k] + jnp.sum(sq.reshape(step_rows // 8, 8, width), axis=0))
            row_acc[pl.ds(at, step_rows), :] = lane
            return tuple(out)

        accs = lax.fori_loop(
            0, rows // step_rows, body, (jnp.zeros((8, width), F32),) * HALVES, unroll=4
        )
        for k in range(HALVES):
            total = jnp.sum(accs[k], axis=0, keepdims=True)
            for g in range(groups):
                line = k * groups + g
                col_buf[p, line : line + 1, :] = total[:, g * LANES : (g + 1) * LANES]

    def send_cols(d):
        peer = lax.rem(me + d, n)
        return pltpu.make_async_remote_copy(
            src_ref=col_buf.at[peer], dst_ref=col_recv.at[d],
            send_sem=col_send.at[d], recv_sem=col_recv_sem.at[d],
            device_id={"fsdp": peer}, device_id_type=MESH,
        )

    for d in range(1, n):
        send_cols(d).start()

    row_line = jnp.sum(jnp.transpose(row_acc[...]), axis=0, keepdims=True)
    row_buf[...] = jnp.zeros_like(row_buf)
    for g in range(row_groups):
        row_buf[g : g + 1, :] = row_line[:, g * LANES : (g + 1) * LANES]
    send_rows = pltpu.make_async_remote_copy(
        src_ref=row_buf, dst_ref=row_recv, send_sem=row_sems.at[0], recv_sem=row_sems.at[1],
        device_id={"tp": 1 - core}, device_id_type=MESH,
    )
    send_rows.start()

    def biggest(c, m):
        wload(c).wait()

        def inner(r, m):
            x = jnp.abs(weight_buf[c, pl.ds(pl.multiple_of(r * 64, 64), 64), :])
            for g in range(groups):
                for k in range(4):
                    m = jnp.maximum(m, x[k * 16 : k * 16 + 16, g * LANES : (g + 1) * LANES])
            return m

        return lax.fori_loop(0, rows // 64, inner, m)

    weight_max = lax.fori_loop(0, chunks, biggest, jnp.zeros((16, LANES), BF16))
    weight_max = jnp.max(weight_max.astype(F32), axis=(0, 1), keepdims=True)

    send_rows.wait()
    row_total = row_buf[...] + row_recv[...]
    new_rows = 0.8 * row_moment_ref[...] + 0.2 * (row_total[:row_groups] / ff + 1e-30)
    rows_ref[...] = new_rows
    rows_summed = jnp.sum(new_rows, axis=(0, 1), keepdims=True)
    rows_least = jnp.min(new_rows, axis=(0, 1), keepdims=True)

    col_total = col_buf[me]
    for d in range(1, n):
        send_cols(d).wait()
        col_total = col_total + col_recv[d]
    msg[0:chunk] = col_total
    msg[chunk : chunk + 8] = jnp.zeros((8, LANES), F32)
    msg[chunk : chunk + 1] = jnp.broadcast_to(rows_summed, (1, LANES))
    msg[chunk + 1 : chunk + 2] = jnp.broadcast_to(rows_least, (1, LANES))
    msg[chunk + 2 : chunk + 3] = jnp.broadcast_to(weight_max, (1, LANES))

    def send_msg(d):
        return pltpu.make_async_remote_copy(
            src_ref=msg, dst_ref=all_buf.at[me],
            send_sem=msg_send.at[d], recv_sem=msg_recv.at[d],
            device_id={"fsdp": lax.rem(me + d, n)}, device_id_type=MESH,
        )

    for d in range(1, n):
        send_msg(d).start()
    all_buf[me] = msg[...]

    for d in range(1, n):
        send_normed(d).wait()
    give = pltpu.make_async_remote_copy(
        src_ref=norm_got.at[core], dst_ref=norm_got.at[core],
        send_sem=pass_sems.at[0], recv_sem=pass_sems.at[1],
        device_id={"tp": 1 - core}, device_id_type=MESH,
    )
    give.start()
    factor = 0.01 * lax.rsqrt(new_rows)
    for g in range(row_groups):
        line = jnp.broadcast_to(factor[g : g + 1, :], (LANES, LANES))
        row_factor[g * LANES : (g + 1) * LANES, :] = jnp.transpose(line)

    for d in range(1, n):
        send_msg(d).wait()
    summed = all_buf[0, chunk : chunk + 1, :]
    least = all_buf[0, chunk + 1 : chunk + 2, :]
    heaviest = all_buf[0, chunk + 2 : chunk + 3, :]
    for o in range(1, n):
        summed = summed + all_buf[o, chunk : chunk + 1, :]
        least = jnp.minimum(least, all_buf[o, chunk + 1 : chunk + 2, :])
        heaviest = jnp.maximum(heaviest, all_buf[o, chunk + 2 : chunk + 3, :])
    row_scale = summed / d_model
    root = jnp.sqrt(row_scale)
    ratio = jnp.zeros((1, LANES), F32)
    for o in range(n):
        here = slice(o * chunk, (o + 1) * chunk)
        sums = all_buf[o, 0:chunk, :]
        new_columns = 0.8 * col_moment_ref[here, :] + 0.2 * (sums / d_model + 1e-30)
        cols_ref[here, :] = new_columns
        scaled = lax.rsqrt(new_columns) * root
        col_factor[o] = scaled
        ratio = jnp.maximum(ratio, jnp.max(sums / new_columns, axis=0, keepdims=True))
    ratio = jnp.max(ratio, axis=1, keepdims=True)

    column_norm = d_model**0.5 * heaviest + 0.01 * jnp.sqrt(row_scale / least * ratio)
    bound = (1.02 * GAIN_MAX * d_model**0.5 * column_norm + 1e-25)[:, 0:1]
    scale = 8000.0 / bound
    unscale = bound / 8000.0
    give.wait()

    place = jnp.where(lax.rem(me, 2) == 0, me // 2, n - 1 - me // 2)

    def device_at(q):
        q = lax.rem(q + n, n)
        return jnp.where(q < n // 2, 2 * q, 2 * (n - 1 - q) + 1)

    neighbours = (device_at(place + 1), device_at(place - 1))

    def copy(way, step, c):
        return pltpu.make_async_remote_copy(
            src_ref=sent.at[way, step, c],
            dst_ref=got.at[way, step, c],
            send_sem=send_sem.at[way, step, c],
            recv_sem=recv_sem.at[way, step, c],
            device_id={"fsdp": neighbours[way]},
            device_id_type=MESH,
        )

    def pass_on(way, step, c, first):
        far = steps - step
        dest = device_at(place + far) if way == 0 else device_at(place - far)
        total = part[c, dest]
        if not first:
            copy(way, step - 1, c).wait_recv()
            total = total + decode(got[way, step - 1, c], unscale)
        sent[way, step, c] = encode(total * scale)
        copy(way, step, c).start()

    @pl.loop(0, n)
    def _(pair):
        for way in range(2):
            c = 2 * pair + way

            @pl.loop(0, row_groups)
            def _(r):
                block = pl.ds(pl.multiple_of(r * LANES, LANES), LANES)
                for g in range(groups):
                    at = slice(g * LANES, (g + 1) * LANES)
                    change = (
                        grad_buf[c, block, at].astype(F32)
                        * row_factor[block, :]
                        * col_factor[pair, way * groups + g : way * groups + g + 1, :]
                    )
                    weight_buf[c, block, at] = (
                        weight_buf[c, block, at].astype(F32) - change
                    ).astype(BF16)

            store(c).start()
            product = jnp.dot(
                norm_got[0].reshape(n * tokens, half), weight_buf[c, :half, :],
                preferred_element_type=F32,
            ) + jnp.dot(
                norm_got[1].reshape(n * tokens, half), weight_buf[c, half:, :],
                preferred_element_type=F32,
            )
            part[c] = product.reshape(n, tokens, width)
            pass_on(way, 0, c, True)
            pass_on(1 - way, 1, c, True)

    @pl.loop(0, n)
    def _(pair):
        for way in range(2):
            pass_on(way, 1, 2 * pair + way, False)

    for step in range(2, steps):

        @pl.loop(0, chunks)
        def _(c):
            for way in range(2):
                pass_on(way, step, c, False)

    @pl.loop(0, chunks)
    def _(c):
        total = part[c, me]
        for way in range(2):
            copy(way, steps - 1, c).wait_recv()
            total = total + decode(got[way, steps - 1, c], unscale)
        up_ref[:, columns(c)] = total.astype(BF16)

    @pl.loop(0, n)
    def _(pair):
        for way in range(2):
            store(2 * pair + way).wait()
            copy(way, 0, 2 * pair + way).wait_send()
            for step in range(1, steps):
                for parity in range(2):
                    copy(way, step, 2 * pair + parity).wait_send()


def finish_kernel(
    made_ref, gate_ref, up_ref, rows_in, cols_in, weight_ref, hidden_ref, rows_out, cols_out,
    out_sem,
):
    pieces = out_sem.shape[0]
    height = made_ref.shape[0] // pieces

    def store(p):
        at = pl.ds(p * height, height)
        return pltpu.make_async_copy(made_ref.at[at, :], weight_ref.at[at, :], out_sem.at[p])

    for p in range(pieces):
        store(p).start()
    rows_out[...] = rows_in[...]
    cols_out[...] = cols_in[...]
    each = gate_ref.shape[1] // pieces
    for p in range(pieces):
        at = slice(p * each, (p + 1) * each)
        gate = gate_ref[:, at].astype(F32)
        silu = gate / (1.0 + jnp.exp(-gate))
        hidden_ref[:, at] = (silu * up_ref[:, at].astype(F32)).astype(BF16)
    for p in range(pieces):
        store(p).wait()


def finish(made, gate, up_values, new_rows, new_columns):
    rows, cols = made.shape
    pieces = 16
    vmem = pl.BlockSpec(memory_space=pltpu.VMEM)
    hbm = pl.BlockSpec(memory_space=pl.ANY)
    return pl.pallas_call(
        finish_kernel,
        out_shape=(
            jax.ShapeDtypeStruct(made.shape, BF16),
            jax.ShapeDtypeStruct(gate.shape, BF16),
            jax.ShapeDtypeStruct(new_rows.shape, F32),
            jax.ShapeDtypeStruct(new_columns.shape, F32),
        ),
        in_specs=[hbm, vmem, vmem, vmem, vmem],
        out_specs=(hbm, vmem, vmem, vmem),
        scratch_shapes=[
            pltpu.SemaphoreType.DMA((pieces,)),
        ],
        compiler_params=pltpu.CompilerParams(vmem_limit_bytes=16 * 1024 * 1024),
        name="finish",
    )(made, gate, up_values, new_rows, new_columns)


def kernels_fit(n, tp, rows, cols, tokens):
    held = 2 * rows * cols * 2 + n * tokens * cols * (4 + 2 + 2) + tokens * cols * 2
    held += 4 * n * tokens * rows * 2 + 2 * tokens * n * rows * 4
    return (
        tp == 2
        and n >= 4
        and rows % (2 * LANES) == 0
        and rows // LANES <= 8
        and cols % (8 * LANES * n) == 0
        and cols % (HALVES * LANES * n) == 0
        and tokens % 16 == 0
        and held <= VMEM_BUDGET - (4 << 20)
    )


def with_kernels(n, ff, d_model, weight, grad, row_moment, col_moment, states, gain, gate):
    rows, cols = grad.shape
    tokens = states.shape[0]
    chunk = cols // n // LANES
    half = rows // 2
    chunks = HALVES * n
    width = cols // chunks
    slots = (2, n // 2, chunks)
    vmem = pl.BlockSpec(memory_space=pltpu.VMEM)
    hbm = pl.BlockSpec(memory_space=pl.ANY)
    shape = jax.ShapeDtypeStruct
    dma = pltpu.SemaphoreType.DMA
    new_weight, new_rows, new_columns, up_values = pl.pallas_call(
        functools.partial(step_kernel, n, ff, d_model),
        out_shape=(
            pltpu.VMEM((rows, cols), BF16),
            shape((rows // LANES, LANES), F32),
            shape((cols // LANES, LANES), F32),
            shape((tokens, cols), BF16),
        ),
        in_specs=[hbm, hbm, vmem, vmem, vmem, vmem],
        out_specs=(hbm, vmem, vmem, vmem),
        scratch_shapes=[
            pltpu.VMEM((chunks, rows, width), BF16),
            pltpu.VMEM((chunks, rows, width), BF16),
            pltpu.VMEM((rows, LANES), F32),
            pltpu.VMEM((8, LANES), F32),
            pltpu.VMEM((8, LANES), F32),
            pltpu.VMEM((n, chunk, LANES), F32),
            pltpu.VMEM((n, chunk, LANES), F32),
            pltpu.VMEM((chunk + 8, LANES), F32),
            pltpu.VMEM((n, chunk + 8, LANES), F32),
            pltpu.VMEM((2, n, tokens, half), BF16),
            pltpu.VMEM((2, n, tokens, half), BF16),
            pltpu.VMEM((rows, LANES), F32),
            pltpu.VMEM((n, chunk, LANES), F32),
            pltpu.VMEM((chunks, n, tokens, width), F32),
            pltpu.VMEM((*slots, tokens, width), BF16),
            pltpu.VMEM((*slots, tokens, width), BF16),
            dma((chunks,)), dma((chunks,)), dma((chunks,)), dma((2,)), dma((n,)), dma((n,)),
            dma((n,)), dma((n,)), dma((n,)), dma((n,)), dma((2,)), dma(slots), dma(slots),
        ],
        compiler_params=pltpu.CompilerParams(
            collective_id=0, has_side_effects=True, vmem_limit_bytes=48 * 1024 * 1024
        ),
        name="whole_step",
    )(
        grad, weight, row_moment.reshape(rows // LANES, LANES),
        col_moment.reshape(cols // LANES, LANES), states, gain.reshape(-1, LANES),
    )
    new_weight, hidden, new_rows, new_columns = finish(
        new_weight, gate, up_values, new_rows, new_columns
    )
    return new_weight, new_rows.reshape(-1), new_columns.reshape(-1), hidden


def with_collectives(ff, d_model, weight, grad, row_moment, col_moment, states, gain, gate):
    gradient = grad.astype(F32)
    squares = gradient * gradient + 1e-30
    row_total = lax.psum(jnp.sum(squares, axis=1), "tp")
    new_rows = 0.8 * row_moment + 0.2 * (row_total / ff)
    col_total, rows_summed = lax.psum((jnp.sum(squares, axis=0), jnp.sum(new_rows)), "fsdp")
    new_columns = 0.8 * col_moment + 0.2 * (col_total / d_model)
    row_scale = rows_summed / d_model
    change = gradient / jnp.sqrt(new_rows[:, None] * new_columns[None, :] / row_scale)
    new_weight = (weight.astype(F32) - 0.01 * change).astype(BF16)
    values = states.astype(F32)
    normed = (
        values
        * lax.rsqrt(jnp.mean(values * values, axis=1, keepdims=True) + 1e-06)
        * gain.astype(F32)
    ).astype(BF16)
    column_block = lax.all_to_all(new_weight, "fsdp", split_axis=1, concat_axis=0, tiled=True)
    up_block = jnp.dot(
        lax.all_gather(normed, "fsdp", axis=0, tiled=True),
        column_block,
        preferred_element_type=F32,
    ).astype(BF16)
    up_values = lax.all_to_all(up_block, "fsdp", split_axis=0, concat_axis=1, tiled=True)
    hidden = (jax.nn.silu(gate.astype(F32)) * up_values.astype(F32)).astype(BF16)
    return new_weight, new_rows, new_columns, hidden


def solution(mesh):
    n, tp = mesh.shape["fsdp"], mesh.shape["tp"]

    def on_device(weight, grad, row_moment, col_moment, states, gain, gate):
        rows, cols = weight.shape
        ff, d_model = cols * tp, rows * n
        arrays = (weight, grad, row_moment, col_moment, states, gain, gate)
        if kernels_fit(n, tp, rows, cols, states.shape[0]):
            return with_kernels(n, ff, d_model, *arrays)
        return with_collectives(ff, d_model, *arrays)

    return jax.shard_map(
        on_device,
        mesh=mesh,
        in_specs=(
            P(("job", "fsdp"), "tp"),
            P(("job", "fsdp"), "tp"),
            P(("job", "fsdp")),
            P(("job", "tp")),
            P(("job", "fsdp"), None),
            P("job"),
            P(("job", "fsdp"), "tp"),
        ),
        out_specs=(
            P(("job", "fsdp"), "tp"),
            P(("job", "fsdp")),
            P(("job", "tp")),
            P(("job", "fsdp"), "tp"),
        ),
        check_vma=False,
    )
```
